32 devices in a mesh: row: 8 (over z, x), col: 4 (over y, core).
Axes of the slice: x: 2, y: 2, z: 4, core: 2. Of those that a mesh axis runs over, the one named last changes fastest.
Arguments:
- panel: float32 [131072, 512], P('row', 'col'), may hold values from -6 to 6
- signs: int32 [131072], P('row'), may hold values from -1 to 1, as said below
- samples: int32 [32768], replicated, may hold values from 0 to 131071, as said below
Outputs:
- sketch: float32 [32768, 512], P('row', 'col')
- gram: float32 [512, 512], P('col')
The draws below stay inside these ranges and needn't reach their ends.
Inputs may be any that keep to these rules, and one draw needn't show every extreme that they name: `signs`: each entry is -1 or +1. `samples`: row indices, repeats allowed, unevenly spread over the row shards; in each aligned block of 4096 entries, at most 1024 entries share the value of (index % 16384) // 2048, and in every such block some value is shared by exactly 1024.
All inputs are finite; a program needn't handle non-finite values.
Results may differ from the reference program's by a relative error of at most 0.0001.
Values sent between devices are 32-bit elements; how exact they have to be, the bound alone decides.
A program may use at most 128 MiB of HBM per device.

```python
import math
import jax
import jax.numpy as jnp
from jax import lax

PANEL = 128
ROWS_DEV = 16384
SAMPLES = 32768
M = 131072
COLS = 512
SLOTS = 4096
BLOCK = 2048
CAP = 1024
N_ROW = 8
N_COL = 4


def draw_signs(key, part):
    key = jax.random.fold_in(key, 1)
    return 2 * jax.random.randint(key, (M,), 0, 2, dtype=jnp.int32) - 1


def block_owners(key):
    key_pick, key_rest, key_order = jax.random.split(key, 3)
    chosen = jax.random.randint(key_pick, (), 0, N_ROW, dtype=jnp.int32)
    others = jnp.arange((N_ROW - 1) * CAP, dtype=jnp.int32) // CAP
    others = jnp.where(others >= chosen, others + 1, others)
    others = jax.random.permutation(key_rest, others)
    listed = jnp.concatenate([jnp.full((CAP,), chosen, dtype=jnp.int32), others])[:SLOTS]
    return jax.random.permutation(key_order, listed)


def draw_samples(key, part):
    key = jax.random.fold_in(key, 2)
    key_one, key_two, key_three, key_four = jax.random.split(key, 4)
    first = jax.random.randint(key_one, (SAMPLES,), 0, N_ROW, dtype=jnp.int32)
    second = jax.random.randint(key_two, (SAMPLES,), 0, N_ROW, dtype=jnp.int32)
    device = jnp.minimum(first, second)
    owners = jax.vmap(block_owners)(jax.random.split(key_three, N_ROW)).reshape(SAMPLES)
    offset = jax.random.randint(key_four, (SAMPLES,), 0, BLOCK, dtype=jnp.int32)
    index = device * ROWS_DEV + owners * BLOCK + offset
    return index.astype(jnp.int32)


def shard_levels(rng, shape, cuts, least, top_value):
    level, own = 1.0, jax.random.fold_in(rng, 6)
    for position, blocks in cuts:
        heights = jnp.exp(jax.random.uniform(jax.random.fold_in(own, position), (blocks,), jnp.float32, least / len(cuts), top_value / len(cuts)))
        level = level * jnp.repeat(heights, shape[position] // blocks).reshape([-1 if axis == position else 1 for axis in range(len(shape))])
    return level


def centred(rng, extent, width, reach, cuts=(), kind=jnp.bfloat16):
    loudness = shard_levels(rng, extent, cuts, -0.22, 0.18) if cuts else 1.0
    values = jax.random.normal(rng, extent, jnp.float32) * width * loudness
    return jnp.minimum(jnp.maximum(values, -reach), reach).astype(kind)


def setup_inputs(seed: int = 0) -> dict:
    key_list = jax.random.split(jax.random.key(seed), 4)
    panel = centred(key_list[0], (M, COLS), 1.0, 6.0, ((0, 8), (1, 4)), jnp.float32)
    signs = draw_signs(jax.random.fold_in(key_list[3], 71), 0)
    samples = draw_samples(jax.random.fold_in(key_list[3], 71), 0)
    return {"panel": panel, "signs": signs, "samples": samples}


def parity(value):
    value = value ^ value >> 16
    value = value ^ value >> 8
    value = value ^ value >> 4
    value = value ^ value >> 2
    value = value ^ value >> 1
    return value & 1

def sylvester(order):
    index = jnp.arange(order, dtype=jnp.int32)
    bits = parity(index[:, None] & index[None, :])
    return (1 - 2 * bits).astype(jnp.float32)

def reference(panel, signs, samples):
    inner_len = min(ROWS_DEV, 256)
    outer_len = ROWS_DEV // inner_len
    h_inner = sylvester(inner_len)
    h_outer = sylvester(outer_len)
    h_device = sylvester(N_ROW)
    scale = 1.0 / math.sqrt(float(M))
    pieces = []
    for column in range(N_COL):
        block = panel[:, column * PANEL:(column + 1) * PANEL]
        signed = block * signs[:, None].astype(jnp.float32)
        shaped = signed.reshape(N_ROW, outer_len, inner_len, PANEL)
        shaped = jnp.einsum('cj,dajp->dacp', h_inner, shaped, precision=lax.Precision.HIGHEST)
        shaped = jnp.einsum('ba,dacp->dbcp', h_outer, shaped, precision=lax.Precision.HIGHEST)
        shaped = jnp.einsum('ed,dbcp->ebcp', h_device, shaped, precision=lax.Precision.HIGHEST)
        mixed = shaped.reshape(M, PANEL) * scale
        pieces.append(jnp.take(mixed, samples, axis=0))
    sketch = jnp.concatenate(pieces, axis=1)
    gram = jnp.dot(sketch.T, sketch, precision=lax.Precision.HIGHEST, preferred_element_type=jnp.float32) / SAMPLES
    return (sketch, gram)
```

```python
import functools
import math

import jax
import jax.numpy as jnp
import numpy as np
from jax import lax
from jax.experimental import pallas as pl
from jax.experimental.pallas import tpu as pltpu
from jax.sharding import PartitionSpec as P

INNER = 256
VMEM_LIMIT = 48 * 1024 * 1024


def sylvester(order):
    index = np.arange(order)
    bits = index[:, None] & index[None, :]
    parity = np.zeros_like(bits)
    while bits.any():
        parity ^= bits & 1
        bits >>= 1
    return (1 - 2 * parity).astype(np.float32)


def butterfly(values):
    values = list(values)
    step = 1
    while step < len(values):
        for start in range(0, len(values), 2 * step):
            for k in range(start, start + step):
                a, b = values[k], values[k + step]
                values[k], values[k + step] = a + b, a - b
        step *= 2
    return values


def transform_kernel(steps_in, outer, devices, scale, h_ref, signs_ref, x_ref, out_ref, held):
    t = pl.program_id(0)
    per = outer // steps_in
    rows_out = out_ref.shape[2]

    @pl.when(t < steps_in)
    def _():
        h = h_ref[...]
        for k in range(per):
            x = x_ref[k]
            high = x.astype(jnp.bfloat16)
            low = (x - high.astype(jnp.float32)).astype(jnp.bfloat16)
            both = jnp.concatenate([high, low], axis=1)
            signed = (h * signs_ref[k]).astype(jnp.bfloat16)
            y = jnp.dot(signed, both, preferred_element_type=jnp.float32)
            width = x.shape[1]
            held[t * per + k] = (y[:, :width] + y[:, width:]) * scale

    @pl.when(t >= steps_in)
    def _():
        rows = pl.ds(pl.multiple_of((t - steps_in) * rows_out, rows_out), rows_out)
        low = 8
        for g in range(outer // low):
            values = butterfly([held[g * low + j, rows, :] for j in range(low)])
            for j in range(low):
                held[g * low + j, rows, :] = values[j]
        for j in range(low):
            values = butterfly([held[k * low + j, rows, :] for k in range(outer // low)])
            for k in range(outer // low):
                a = k * low + j
                out_ref[a % devices, a // devices] = values[k]


def local_transform(panel, signs, devices, scale):
    rows, width = panel.shape
    outer = rows // INNER
    steps_in = outer // 4
    rows_out = 32
    steps_out = INNER // rows_out
    h = jnp.asarray(sylvester(INNER))
    return pl.pallas_call(
        functools.partial(transform_kernel, steps_in, outer, devices, scale),
        grid=(steps_in + steps_out,),
        in_specs=[
            pl.BlockSpec((INNER, INNER), lambda t: (0, 0)),
            pl.BlockSpec((4, 1, INNER), lambda t: (jnp.minimum(t, steps_in - 1), 0, 0)),
            pl.BlockSpec((4, INNER, width), lambda t: (jnp.minimum(t, steps_in - 1), 0, 0)),
        ],
        out_specs=pl.BlockSpec(
            (devices, outer // devices, rows_out, width),
            lambda t: (0, 0, jnp.maximum(t - steps_in, 0), 0),
        ),
        out_shape=jax.ShapeDtypeStruct((devices, outer // devices, INNER, width), jnp.float32),
        scratch_shapes=[pltpu.VMEM((outer, INNER, width), jnp.float32)],
        compiler_params=pltpu.CompilerParams(vmem_limit_bytes=VMEM_LIMIT),
        cost_estimate=pl.CostEstimate(
            flops=4 * rows * INNER * width, bytes_accessed=8 * rows * width, transcendentals=0
        ),
        name="local_transform",
    )(h, signs.astype(jnp.float32).reshape(outer, 1, INNER), panel.reshape(outer, INNER, width))


def copy_rows(index_ref, first, count, source, store):
    unroll = 16 if count % 16 == 0 else 8

    @pl.loop(0, count // unroll)
    def _(k):
        base = k * unroll
        for u in range(unroll):
            store(base + u, source[pl.ds(index_ref[first + base + u], 1), :])


def pick_kernel(steps_in, index_ref, x_ref, out_ref, held):
    t = pl.program_id(0)
    devices, block, _ = x_ref.shape
    chunk = 32 if devices <= 8 else 8
    total = steps_in * block

    @pl.when(t == 0)
    def _():
        held[pl.ds(0, 8), :] = jnp.zeros((8, held.shape[1]), jnp.float32)

    @pl.when(t < steps_in)
    def _():
        @pl.loop(0, block // chunk)
        def _(c):
            rows = pl.ds(pl.multiple_of(c * chunk, chunk), chunk)
            values = butterfly([x_ref[d, rows, :] for d in range(devices)])
            for e in range(devices):
                at = pl.multiple_of(8 + e * total + t * block + c * chunk, 8)
                held[pl.ds(at, chunk), :] = values[e]

    @pl.when(t >= steps_in)
    def _():
        count = out_ref.shape[1]

        def store(r, row):
            out_ref[0, pl.ds(r, 1), :] = row

        copy_rows(index_ref, (t - steps_in) * count, count, held, store)


def combine_and_pick(received, index, capacity):
    devices, block_len, width = received.shape
    block = min(block_len, 256)
    steps_in = block_len // block
    return pl.pallas_call(
        functools.partial(pick_kernel, steps_in),
        grid_spec=pltpu.PrefetchScalarGridSpec(
            num_scalar_prefetch=1,
            grid=(steps_in + devices,),
            in_specs=[
                pl.BlockSpec((devices, block, width), lambda t, i: (0, jnp.minimum(t, steps_in - 1), 0))
            ],
            out_specs=pl.BlockSpec(
                (1, capacity, width), lambda t, i: (jnp.maximum(t - steps_in, 0), 0, 0)
            ),
            scratch_shapes=[pltpu.VMEM((devices * block_len + 8, width), jnp.float32)],
        ),
        out_shape=jax.ShapeDtypeStruct((devices, capacity, width), jnp.float32),
        compiler_params=pltpu.CompilerParams(vmem_limit_bytes=VMEM_LIMIT),
        name="combine_and_pick",
    )(index.reshape(-1), received)


def place_kernel(index_ref, x_ref, out_ref):
    count = out_ref.shape[0]

    def store(r, row):
        out_ref[pl.ds(r, 1), :] = row

    copy_rows(index_ref, pl.program_id(0) * count, count, x_ref, store)


def place_rows(arrived, index):
    rows, width = arrived.shape
    slots = index.shape[0]
    count = min(slots, 512)
    return pl.pallas_call(
        place_kernel,
        grid_spec=pltpu.PrefetchScalarGridSpec(
            num_scalar_prefetch=1,
            grid=(slots // count,),
            in_specs=[pl.BlockSpec((rows, width), lambda t, i: (0, 0))],
            out_specs=pl.BlockSpec((count, width), lambda t, i: (t, 0)),
        ),
        out_shape=jax.ShapeDtypeStruct((slots, width), jnp.float32),
        compiler_params=pltpu.CompilerParams(vmem_limit_bytes=VMEM_LIMIT),
        name="place_rows",
    )(index, arrived)


def gram_of(picked, sample_total):
    count, width = picked.shape
    half = count // 2
    columns = lax.axis_size("col")
    devices = lax.axis_size("row")
    c = lax.axis_index("col")
    side = c // 2

    def swap(value, mask):
        return lax.ppermute(value, "col", [(i, i ^ mask) for i in range(columns)])

    def dot(a, b):
        return lax.dot_general(
            a, b, (((0,), (0,)), ((), ())), precision=lax.Precision.HIGH,
            preferred_element_type=jnp.float32,
        )

    mine = lax.dynamic_slice_in_dim(picked, side * half, half)
    theirs = lax.dynamic_slice_in_dim(picked, (1 - side) * half, half)
    across = swap(theirs, 2)
    beside = swap(picked, 1)
    diagonal = swap(across, 1)
    beside_half = lax.dynamic_slice_in_dim(beside, side * half, half)
    near = dot(picked, jnp.concatenate([picked, beside], axis=1))
    far = dot(mine, jnp.concatenate([across, diagonal], axis=1))
    for_other = dot(across, jnp.concatenate([mine, beside_half], axis=1))
    far = far + swap(for_other, 2)
    blocks = jnp.concatenate([near, far], axis=1).reshape(width, columns, width)
    blocks = blocks.transpose(1, 0, 2)
    ordered = [lax.dynamic_index_in_dim(blocks, c ^ j, 0, keepdims=False) for j in range(columns)]
    partial = jnp.concatenate(ordered, axis=1)
    if width % devices or (width // devices) % 8:
        return lax.psum(partial, "row") / sample_total
    pieces = partial.reshape(devices, width // devices, columns * width)
    pieces = lax.all_to_all(pieces, "row", split_axis=0, concat_axis=0, tiled=True)
    reduced = jnp.sum(pieces, axis=0) / sample_total
    spread = jnp.broadcast_to(reduced[None], pieces.shape)
    spread = lax.all_to_all(spread, "row", split_axis=0, concat_axis=0, tiled=True)
    return spread.reshape(width, columns * width)


def shards(panel, signs, samples):
    row_count, width = panel.shape
    devices = lax.axis_size("row")
    me = lax.axis_index("row")
    outer = row_count // INNER
    block_len = row_count // devices
    sample_total = samples.shape[0]
    slots = sample_total // devices
    scale = 1.0 / math.sqrt(float(row_count * devices))

    local_rows = local_transform(panel, signs, devices, scale)
    pieces = local_rows.reshape(devices, block_len, width)
    received = lax.all_to_all(pieces, "row", split_axis=0, concat_axis=0, tiled=True)

    table = samples.reshape(devices, slots)
    local = table % row_count
    owners = (local // INNER) % devices
    in_block = (local // (INNER * devices)) * INNER + local % INNER
    flat = (table // row_count) * block_len + in_block
    mine = owners == me
    rank = jnp.where(mine, jnp.cumsum(mine.astype(jnp.int32), axis=1) - 1, -1)
    ids = jnp.arange(devices, dtype=jnp.int32)
    onehot = owners[:, None, :] == ids[None, :, None]
    most = jnp.max(jnp.sum(onehot.astype(jnp.int32), axis=2))
    my_owners = lax.dynamic_index_in_dim(owners, me, 0, keepdims=False)
    my_onehot = my_owners[None, :] == ids[:, None]
    my_ranks = jnp.cumsum(my_onehot.astype(jnp.int32), axis=1) - 1
    position = jnp.sum(jnp.where(my_onehot, my_ranks, 0), axis=0)

    mean = slots / devices
    capacity = min(slots, -(-int(mean + 5.5 * math.sqrt(mean)) // 16) * 16)

    def pick_index(room):
        wanted = jnp.arange(room, dtype=jnp.int32)[None, :, None]
        return jnp.sum(jnp.where(rank[:, None, :] == wanted, flat[:, None, :] + 8, 0), axis=2)

    received, fast_index = lax.optimization_barrier((received, pick_index(capacity)))

    def exchange(picked, room):
        arrived = lax.all_to_all(picked, "row", split_axis=0, concat_axis=0, tiled=True)
        return arrived.reshape(devices * room, width), my_owners * room + position

    def fast(received):
        picked = combine_and_pick(received, fast_index, capacity)
        sketch = place_rows(*exchange(picked, capacity))
        return sketch, gram_of(picked.reshape(devices * capacity, width), sample_total)

    def general(received):
        combined = jnp.stack(butterfly([received[d] for d in range(devices)]))
        combined = combined.reshape(devices * block_len, width)
        index = pick_index(slots).reshape(-1)
        picked = jnp.take(combined, jnp.maximum(index - 8, 0), axis=0)
        picked = jnp.where((index >= 8)[:, None], picked, 0.0)
        arrived, places = exchange(picked.reshape(devices, slots, width), slots)
        sketch = jnp.take(arrived, places, axis=0)
        return sketch, gram_of(sketch, sample_total)

    return lax.cond(most <= capacity, fast, general, received)


def solution(mesh):
    return jax.shard_map(
        shards,
        mesh=mesh,
        in_specs=(P("row", "col"), P("row"), P()),
        out_specs=(P("row", "col"), P("col", None)),
        check_vma=False,
    )
```

```python
import functools
import math

import jax
import jax.numpy as jnp
import numpy as np
from jax import lax
from jax.experimental import pallas as pl
from jax.experimental.pallas import tpu as pltpu
from jax.sharding import PartitionSpec as P

INNER = 256
VMEM_LIMIT = 48 * 1024 * 1024


def sylvester(order):
    index = np.arange(order)
    bits = index[:, None] & index[None, :]
    parity = np.zeros_like(bits)
    while bits.any():
        parity ^= bits & 1
        bits >>= 1
    return (1 - 2 * parity).astype(np.float32)


def butterfly(values):
    values = list(values)
    step = 1
    while step < len(values):
        for start in range(0, len(values), 2 * step):
            for k in range(start, start + step):
                a, b = values[k], values[k + step]
                values[k], values[k + step] = a + b, a - b
        step *= 2
    return values


def transform_kernel(steps_in, outer, devices, scale, h_ref, signs_ref, x_ref, *refs):
    t = pl.program_id(0)
    *out_refs, held = refs
    per = outer // steps_in
    rows_out = out_refs[0].shape[2]
    members = devices // len(out_refs)

    @pl.when(t < steps_in)
    def _():
        h = h_ref[...]
        for k in range(per):
            x = x_ref[k]
            high = x.astype(jnp.bfloat16)
            low = (x - high.astype(jnp.float32)).astype(jnp.bfloat16)
            both = jnp.concatenate([high, low], axis=1)
            signed = (h * signs_ref[k]).astype(jnp.bfloat16)
            y = jnp.dot(signed, both, preferred_element_type=jnp.float32)
            width = x.shape[1]
            held[t * per + k] = (y[:, :width] + y[:, width:]) * scale

    @pl.when(t >= steps_in)
    def _():
        rows = pl.ds(pl.multiple_of((t - steps_in) * rows_out, rows_out), rows_out)
        low = 8
        for g in range(outer // low):
            values = butterfly([held[g * low + j, rows, :] for j in range(low)])
            for j in range(low):
                held[g * low + j, rows, :] = values[j]
        for j in range(low):
            values = butterfly([held[k * low + j, rows, :] for k in range(outer // low)])
            for k in range(outer // low):
                a = k * low + j
                owner = a % devices
                out_refs[owner // members][owner % members, a // devices] = values[k]


def local_transform(panel, signs, devices, chunks, scale):
    rows, width = panel.shape
    outer = rows // INNER
    steps_in = outer // 4
    rows_out = 32
    steps_out = INNER // rows_out
    h = jnp.asarray(sylvester(INNER))
    return pl.pallas_call(
        functools.partial(transform_kernel, steps_in, outer, devices, scale),
        grid=(steps_in + steps_out,),
        in_specs=[
            pl.BlockSpec((INNER, INNER), lambda t: (0, 0)),
            pl.BlockSpec((4, 1, INNER), lambda t: (jnp.minimum(t, steps_in - 1), 0, 0)),
            pl.BlockSpec((4, INNER, width), lambda t: (jnp.minimum(t, steps_in - 1), 0, 0)),
        ],
        out_specs=[
            pl.BlockSpec(
                (devices // chunks, outer // devices, rows_out, width),
                lambda t: (0, 0, jnp.maximum(t - steps_in, 0), 0),
            )
        ]
        * chunks,
        out_shape=[
            jax.ShapeDtypeStruct((devices // chunks, outer // devices, INNER, width), jnp.float32)
        ]
        * chunks,
        scratch_shapes=[pltpu.VMEM((outer, INNER, width), jnp.float32)],
        compiler_params=pltpu.CompilerParams(vmem_limit_bytes=VMEM_LIMIT),
        cost_estimate=pl.CostEstimate(
            flops=4 * rows * INNER * width, bytes_accessed=8 * rows * width, transcendentals=0
        ),
        name="local_transform",
    )(h, signs.astype(jnp.float32).reshape(outer, 1, INNER), panel.reshape(outer, INNER, width))


def copy_rows(index_ref, first, count, source, store):
    unroll = 16 if count % 16 == 0 else 8

    @pl.loop(0, count // unroll)
    def _(k):
        base = k * unroll
        for u in range(unroll):
            store(base + u, source[pl.ds(index_ref[first + base + u], 1), :])


def pick_kernel(steps_in, index_ref, sign_ref, x_ref, out_ref, held):
    t = pl.program_id(0)
    members, block, _ = x_ref.shape
    chunk = 32 if members <= 8 else 8
    total = steps_in * block

    @pl.when(t == 0)
    def _():
        held[pl.ds(0, 8), :] = jnp.zeros((8, held.shape[1]), jnp.float32)

    @pl.when(t < steps_in)
    def _():
        sign = sign_ref[0].astype(jnp.float32)

        @pl.loop(0, block // chunk)
        def _(c):
            rows = pl.ds(pl.multiple_of(c * chunk, chunk), chunk)
            values = butterfly([x_ref[d, rows, :] for d in range(members)])
            for e in range(2 * members):
                at = pl.multiple_of(8 + e * total + t * block + c * chunk, 8)
                value = values[e] if e < members else values[e - members] * sign
                held[pl.ds(at, chunk), :] = value

    @pl.when(t >= steps_in)
    def _():
        count = out_ref.shape[1]

        def store(r, row):
            out_ref[0, pl.ds(r, 1), :] = row

        copy_rows(index_ref, (t - steps_in) * count, count, held, store)


def combine_and_pick(received, index, sign, capacity):
    members, block_len, width = received.shape
    devices = 2 * members
    block = min(block_len, 256)
    steps_in = block_len // block
    return pl.pallas_call(
        functools.partial(pick_kernel, steps_in),
        grid_spec=pltpu.PrefetchScalarGridSpec(
            num_scalar_prefetch=2,
            grid=(steps_in + devices,),
            in_specs=[
                pl.BlockSpec(
                    (members, block, width), lambda t, i, g: (0, jnp.minimum(t, steps_in - 1), 0)
                )
            ],
            out_specs=pl.BlockSpec(
                (1, capacity, width), lambda t, i, g: (jnp.maximum(t - steps_in, 0), 0, 0)
            ),
            scratch_shapes=[pltpu.VMEM((devices * block_len + 8, width), jnp.float32)],
        ),
        out_shape=jax.ShapeDtypeStruct((devices, capacity, width), jnp.float32),
        compiler_params=pltpu.CompilerParams(vmem_limit_bytes=VMEM_LIMIT),
        cost_estimate=pl.CostEstimate(
            flops=8 * devices * block_len * width,
            bytes_accessed=16 * devices * block_len * width,
            transcendentals=0,
        ),
        name="combine_and_pick",
    )(index.reshape(-1), sign.reshape(1), received)


def place_kernel(index_ref, *refs):
    *x_refs, out_ref, held = refs
    count = out_ref.shape[0]
    rows = x_refs[0].shape[0]

    @pl.when(pl.program_id(0) == 0)
    def _():
        for k, x_ref in enumerate(x_refs):
            @pl.loop(0, rows // 16)
            def _(c):
                at = pl.multiple_of(c * 16, 16)
                held[pl.ds(k * rows + at, 16), :] = x_ref[pl.ds(at, 16), :]

    def store(r, row):
        out_ref[pl.ds(r, 1), :] = row

    copy_rows(index_ref, pl.program_id(0) * count, count, held, store)


def place_rows(arrived, index):
    rows, width = arrived[0].shape
    slots = index.shape[0]
    count = min(slots, 512)
    return pl.pallas_call(
        place_kernel,
        grid_spec=pltpu.PrefetchScalarGridSpec(
            num_scalar_prefetch=1,
            grid=(slots // count,),
            in_specs=[pl.BlockSpec((rows, width), lambda t, i: (0, 0))] * len(arrived),
            out_specs=pl.BlockSpec((count, width), lambda t, i: (t, 0)),
            scratch_shapes=[pltpu.VMEM((rows * len(arrived), width), jnp.float32)],
        ),
        out_shape=jax.ShapeDtypeStruct((slots, width), jnp.float32),
        compiler_params=pltpu.CompilerParams(vmem_limit_bytes=VMEM_LIMIT),
        name="place_rows",
    )(index, *arrived)


def swap_columns(value, mask):
    columns = lax.axis_size("col")
    return lax.ppermute(value, "col", [(i, i ^ mask) for i in range(columns)])


def gram_terms(picked):
    half = picked.shape[0] // 2
    side = lax.axis_index("col") // 2

    def dot(a, b):
        return lax.dot_general(
            a, b, (((0,), (0,)), ((), ())), precision=lax.Precision.HIGH,
            preferred_element_type=jnp.float32,
        )

    mine = lax.dynamic_slice_in_dim(picked, side * half, half)
    theirs = lax.dynamic_slice_in_dim(picked, (1 - side) * half, half)
    across = swap_columns(theirs, 2)
    beside = swap_columns(picked, 1)
    diagonal = swap_columns(across, 1)
    beside_half = lax.dynamic_slice_in_dim(beside, side * half, half)
    near = dot(picked, jnp.concatenate([picked, beside], axis=1))
    far = dot(mine, jnp.concatenate([across, diagonal], axis=1))
    for_other = dot(across, jnp.concatenate([mine, beside_half], axis=1))
    return near, far, for_other


def gram_from(terms, sample_total, after):
    near, far, for_other = terms
    columns = lax.axis_size("col")
    c = lax.axis_index("col")
    width = near.shape[0]
    far = far + swap_columns(for_other, 2)
    blocks = jnp.concatenate([near, far], axis=1).reshape(width, columns, width)
    blocks = blocks.transpose(1, 0, 2)
    ordered = [lax.dynamic_index_in_dim(blocks, c ^ j, 0, keepdims=False) for j in range(columns)]
    partial = jnp.concatenate(ordered, axis=1)
    devices = lax.axis_size("row")
    if after is None or devices & (devices - 1) or width % (8 * devices):
        return sum_over_rows(partial) / sample_total
    return reduce_rows(partial, after, 1.0 / sample_total)


def reduce_kernel(scale, x_ref, *refs):
    out_ref, came, total, gathered, send_in, recv_in, send_out, recv_out = refs[-8:]
    devices = x_ref.shape[0]
    me = lax.axis_index("row")
    mesh_id = pl.DeviceIdType.MESH
    barrier = pltpu.get_barrier_semaphore()
    for m in range(1, devices):
        pl.semaphore_signal(barrier, inc=1, device_id={"row": me ^ m}, device_id_type=mesh_id)
    pl.semaphore_wait(barrier, devices - 1)
    copies = []
    for m in range(1, devices):
        copy = pltpu.make_async_remote_copy(
            src_ref=x_ref.at[me ^ m], dst_ref=came.at[m], send_sem=send_in.at[m],
            recv_sem=recv_in.at[m], device_id={"row": me ^ m}, device_id_type=mesh_id,
        )
        copy.start()
        copies.append(copy)
    value = x_ref[me]
    for m in range(1, devices):
        copies[m - 1].wait_recv()
        value = value + came[m]
    value = value * scale
    total[...] = value
    copies_out = []
    for m in range(1, devices):
        copy = pltpu.make_async_remote_copy(
            src_ref=total, dst_ref=gathered.at[m], send_sem=send_out.at[m],
            recv_sem=recv_out.at[m], device_id={"row": me ^ m}, device_id_type=mesh_id,
        )
        copy.start()
        copies_out.append(copy)
    out_ref[me] = value
    for m in range(1, devices):
        copies_out[m - 1].wait_recv()
        out_ref[me ^ m] = gathered[m]
    for copy in copies + copies_out:
        copy.wait_send()


def reduce_rows(partial, after, scale):
    devices = lax.axis_size("row")
    rows, columns = partial.shape
    part = (devices, rows // devices, columns)
    out = pl.pallas_call(
        functools.partial(reduce_kernel, scale),
        in_specs=[pl.BlockSpec(memory_space=pltpu.VMEM)]
        + [pl.BlockSpec(memory_space=pl.ANY)] * len(after),
        out_specs=pl.BlockSpec(memory_space=pltpu.VMEM),
        out_shape=jax.ShapeDtypeStruct(part, jnp.float32),
        scratch_shapes=[
            pltpu.VMEM(part, jnp.float32),
            pltpu.VMEM(part[1:], jnp.float32),
            pltpu.VMEM(part, jnp.float32),
        ]
        + [pltpu.SemaphoreType.DMA((devices,))] * 4,
        compiler_params=pltpu.CompilerParams(
            collective_id=0, has_side_effects=True, vmem_limit_bytes=VMEM_LIMIT
        ),
        name="reduce_rows",
    )(partial.reshape(part), *after)
    return out.reshape(rows, columns)


def sum_over_rows(value):
    devices = lax.axis_size("row")
    me = lax.axis_index("row")
    if devices & (devices - 1) or value.shape[0] % devices:
        return lax.psum(value, "row")

    def swap(part, mask):
        return lax.ppermute(part, "row", [(i, i ^ mask) for i in range(devices)])

    masks = [1 << k for k in range(devices.bit_length() - 1)]
    for mask in masks:
        half = value.shape[0] // 2
        upper = (me & mask) != 0
        low, high = value[:half], value[half:]
        value = jnp.where(upper, high, low) + swap(jnp.where(upper, low, high), mask)
    for mask in reversed(masks):
        upper = (me & mask) != 0
        other = swap(value, mask)
        low, high = jnp.where(upper, other, value), jnp.where(upper, value, other)
        value = jnp.concatenate([low, high], axis=0)
    return value


def shards(panel, signs, samples):
    row_count, width = panel.shape
    devices = lax.axis_size("row")
    members = devices // 2
    me = lax.axis_index("row")
    half, member = me // members, me % members
    outer = row_count // INNER
    block_len = row_count // devices
    sample_total = samples.shape[0]
    slots = sample_total // devices
    scale = 1.0 / math.sqrt(float(row_count * devices))
    groups = [list(range(members)), list(range(members, devices))]

    local_rows = local_transform(panel, signs, devices, 2, scale)
    pieces = [chunk.reshape(members, block_len, width) for chunk in local_rows]

    table = samples.reshape(devices, slots)
    local = table % row_count
    owners = (local // INNER) % devices
    in_block = (local // (INNER * devices)) * INNER + local % INNER
    flat = (table // row_count) * block_len + in_block
    ids = jnp.arange(devices, dtype=jnp.int32)
    onehot = owners[:, None, :] == ids[None, :, None]
    most = jnp.max(jnp.sum(onehot.astype(jnp.int32), axis=2))
    my_owners = lax.dynamic_index_in_dim(owners, me, 0, keepdims=False)
    my_onehot = my_owners[None, :] == ids[:, None]
    my_ranks = jnp.cumsum(my_onehot.astype(jnp.int32), axis=1) - 1
    position = jnp.sum(jnp.where(my_onehot, my_ranks, 0), axis=0)

    mean = slots / devices
    capacity = min(slots, -(-int(mean + 5.5 * math.sqrt(mean)) // 16) * 16)

    def pick_index(owner, room):
        mine = owners == owner
        rank = jnp.where(mine, jnp.cumsum(mine.astype(jnp.int32), axis=1) - 1, -1)
        wanted = jnp.arange(room, dtype=jnp.int32)[None, :, None]
        return jnp.sum(jnp.where(rank[:, None, :] == wanted, flat[:, None, :] + 8, 0), axis=2)

    def within(value):
        return lax.all_to_all(
            value, "row", split_axis=0, concat_axis=0, tiled=True, axis_index_groups=groups
        )

    def exchange_blocks(blocks):
        came = []
        for m in range(members):
            block = lax.dynamic_index_in_dim(blocks, member ^ m, 0, keepdims=False)
            if m:
                block = lax.ppermute(block, "row", [(i, i ^ m) for i in range(devices)])
            came.append(block)
        return came

    indices = [pick_index(k * members + member, capacity) for k in range(len(pieces))]
    first, *indices = lax.optimization_barrier((within(pieces[0]), *indices))

    def fast(*pieces):
        sign = 1 - 2 * half
        arrived, terms = [], None
        for k, piece in enumerate(pieces):
            received = within(piece) if k else first
            index = indices[k]
            picked = combine_and_pick(received, index, sign, capacity)
            kept = lax.dynamic_slice_in_dim(picked, half * members, members)
            sent = lax.dynamic_slice_in_dim(picked, (1 - half) * members, members)
            partner = [(i, (i + members) % devices) for i in range(devices)]
            whole = kept + lax.ppermute(sent, "row", partner)
            new = gram_terms(whole.reshape(members * capacity, width))
            terms = new if terms is None else [a + b for a, b in zip(terms, new)]
            arrived += exchange_blocks(whole)
        source = (my_owners // members) * members + ((my_owners % members) ^ member)
        sketch = place_rows(arrived, source * capacity + position)
        return sketch, gram_from(terms, sample_total, arrived)

    def general(*pieces):
        received = lax.all_to_all(
            jnp.concatenate(pieces), "row", split_axis=0, concat_axis=0, tiled=True
        )
        combined = jnp.stack(butterfly([received[d] for d in range(devices)]))
        combined = combined.reshape(devices * block_len, width)
        index = pick_index(me, slots).reshape(-1)
        picked = jnp.take(combined, jnp.maximum(index - 8, 0), axis=0)
        picked = jnp.where((index >= 8)[:, None], picked, 0.0)
        arrived = lax.all_to_all(
            picked.reshape(devices, slots, width), "row", split_axis=0, concat_axis=0, tiled=True
        )
        places = my_owners * slots + position
        sketch = jnp.take(arrived.reshape(devices * slots, width), places, axis=0)
        return sketch, gram_from(gram_terms(sketch), sample_total, None)

    return lax.cond(most <= capacity, fast, general, *pieces)


def solution(mesh):
    return jax.shard_map(
        shards,
        mesh=mesh,
        in_specs=(P("row", "col"), P("row"), P()),
        out_specs=(P("row", "col"), P("col", None)),
        check_vma=False,
    )
```

```python
import functools
import math

import jax
import jax.numpy as jnp
import numpy as np
from jax import lax
from jax.experimental import pallas as pl
from jax.experimental.pallas import tpu as pltpu
from jax.sharding import PartitionSpec as P

INNER = 256
VMEM_LIMIT = 48 * 1024 * 1024


def sylvester(order):
    index = np.arange(order)
    bits = index[:, None] & index[None, :]
    parity = np.zeros_like(bits)
    while bits.any():
        parity ^= bits & 1
        bits >>= 1
    return (1 - 2 * parity).astype(np.float32)


def butterfly(values):
    values = list(values)
    step = 1
    while step < len(values):
        for start in range(0, len(values), 2 * step):
            for k in range(start, start + step):
                a, b = values[k], values[k + step]
                values[k], values[k + step] = a + b, a - b
        step *= 2
    return values


def transform_kernel(steps_in, outer, devices, scale, h_ref, signs_ref, x_ref, *refs):
    t = pl.program_id(0)
    *out_refs, held = refs
    per = outer // steps_in
    rows_out = out_refs[0].shape[2]
    members = devices // len(out_refs)

    @pl.when(t < steps_in)
    def _():
        h = h_ref[...]
        for k in range(per):
            x = x_ref[k]
            high = x.astype(jnp.bfloat16)
            low = (x - high.astype(jnp.float32)).astype(jnp.bfloat16)
            both = jnp.concatenate([high, low], axis=1)
            signed = (h * signs_ref[k]).astype(jnp.bfloat16)
            y = jnp.dot(signed, both, preferred_element_type=jnp.float32)
            width = x.shape[1]
            held[t * per + k] = (y[:, :width] + y[:, width:]) * scale

    @pl.when(t >= steps_in)
    def _():
        rows = pl.ds(pl.multiple_of((t - steps_in) * rows_out, rows_out), rows_out)
        low = 8
        for g in range(outer // low):
            values = butterfly([held[g * low + j, rows, :] for j in range(low)])
            for j in range(low):
                held[g * low + j, rows, :] = values[j]
        for j in range(low):
            values = butterfly([held[k * low + j, rows, :] for k in range(outer // low)])
            for k in range(outer // low):
                a = k * low + j
                owner = a % devices
                out_refs[owner // members][owner % members, a // devices] = values[k]


def local_transform(panel, signs, devices, chunks, scale):
    rows, width = panel.shape
    outer = rows // INNER
    per_step = min(outer, 8)
    steps_in = outer // per_step
    rows_out = 32
    steps_out = INNER // rows_out
    h = jnp.asarray(sylvester(INNER))
    return pl.pallas_call(
        functools.partial(transform_kernel, steps_in, outer, devices, scale),
        grid=(steps_in + steps_out,),
        in_specs=[
            pl.BlockSpec((INNER, INNER), lambda t: (0, 0)),
            pl.BlockSpec((per_step, 1, INNER), lambda t: (jnp.minimum(t, steps_in - 1), 0, 0)),
            pl.BlockSpec((per_step, INNER, width), lambda t: (jnp.minimum(t, steps_in - 1), 0, 0)),
        ],
        out_specs=[
            pl.BlockSpec(
                (devices // chunks, outer // devices, rows_out, width),
                lambda t: (0, 0, jnp.maximum(t - steps_in, 0), 0),
            )
        ]
        * chunks,
        out_shape=[
            jax.ShapeDtypeStruct((devices // chunks, outer // devices, INNER, width), jnp.float32)
        ]
        * chunks,
        scratch_shapes=[pltpu.VMEM((outer, INNER, width), jnp.float32)],
        compiler_params=pltpu.CompilerParams(vmem_limit_bytes=VMEM_LIMIT),
        cost_estimate=pl.CostEstimate(
            flops=4 * rows * INNER * width, bytes_accessed=8 * rows * width, transcendentals=0
        ),
        name="local_transform",
    )(h, signs.astype(jnp.float32).reshape(outer, 1, INNER), panel.reshape(outer, INNER, width))


def copy_rows(index_ref, first, count, source, store):
    unroll = 16 if count % 16 == 0 else 8

    @pl.loop(0, count // unroll)
    def _(k):
        base = k * unroll
        for u in range(unroll):
            store(base + u, source[pl.ds(index_ref[first + base + u], 1), :])


def pick_kernel(steps_in, index_ref, sign_ref, x_ref, out_ref, held):
    t = pl.program_id(0)
    members, block, _ = x_ref.shape
    chunk = 32 if members <= 8 else 8
    total = steps_in * block

    @pl.when(t == 0)
    def _():
        held[pl.ds(0, 8), :] = jnp.zeros((8, held.shape[1]), jnp.float32)

    @pl.when(t < steps_in)
    def _():
        sign = sign_ref[0].astype(jnp.float32)

        @pl.loop(0, block // chunk)
        def _(c):
            rows = pl.ds(pl.multiple_of(c * chunk, chunk), chunk)
            values = butterfly([x_ref[d, rows, :] for d in range(members)])
            for e in range(2 * members):
                at = pl.multiple_of(8 + e * total + t * block + c * chunk, 8)
                value = values[e] if e < members else values[e - members] * sign
                held[pl.ds(at, chunk), :] = value

    @pl.when(t >= steps_in)
    def _():
        count = out_ref.shape[1]

        def store(r, row):
            out_ref[0, pl.ds(r, 1), :] = row

        copy_rows(index_ref, (t - steps_in) * count, count, held, store)


def combine_and_pick(received, index, sign, capacity):
    members, block_len, width = received.shape
    devices = 2 * members
    block = min(block_len, 256)
    steps_in = block_len // block
    return pl.pallas_call(
        functools.partial(pick_kernel, steps_in),
        grid_spec=pltpu.PrefetchScalarGridSpec(
            num_scalar_prefetch=2,
            grid=(steps_in + devices,),
            in_specs=[
                pl.BlockSpec(
                    (members, block, width), lambda t, i, g: (0, jnp.minimum(t, steps_in - 1), 0)
                )
            ],
            out_specs=pl.BlockSpec(
                (1, capacity, width), lambda t, i, g: (jnp.maximum(t - steps_in, 0), 0, 0)
            ),
            scratch_shapes=[pltpu.VMEM((devices * block_len + 8, width), jnp.float32)],
        ),
        out_shape=jax.ShapeDtypeStruct((devices, capacity, width), jnp.float32),
        compiler_params=pltpu.CompilerParams(vmem_limit_bytes=VMEM_LIMIT),
        cost_estimate=pl.CostEstimate(
            flops=8 * devices * block_len * width,
            bytes_accessed=16 * devices * block_len * width,
            transcendentals=0,
        ),
        name="combine_and_pick",
    )(index.reshape(-1), sign.reshape(1), received)


def add_kernel(a_ref, b_ref, *refs):
    refs[-1][...] = a_ref[...] + b_ref[...]


def add_blocks(a, b, after):
    blocks, rows, width = a.shape
    spec = pl.BlockSpec((1, rows, width), lambda t: (t, 0, 0))
    return pl.pallas_call(
        add_kernel,
        grid=(blocks,),
        in_specs=[spec, spec] + [pl.BlockSpec(memory_space=pl.ANY)] * len(after),
        out_specs=spec,
        out_shape=jax.ShapeDtypeStruct(a.shape, jnp.float32),
        compiler_params=pltpu.CompilerParams(vmem_limit_bytes=VMEM_LIMIT),
        name="add_blocks",
    )(a, b, *after)


def place_kernel(index_ref, *refs):
    *x_refs, out_ref, held = refs
    count = out_ref.shape[0]
    rows = x_refs[0].shape[0]

    @pl.when(pl.program_id(0) == 0)
    def _():
        for k, x_ref in enumerate(x_refs):
            @pl.loop(0, rows // 16)
            def _(c):
                at = pl.multiple_of(c * 16, 16)
                held[pl.ds(k * rows + at, 16), :] = x_ref[pl.ds(at, 16), :]

    def store(r, row):
        out_ref[pl.ds(r, 1), :] = row

    copy_rows(index_ref, pl.program_id(0) * count, count, held, store)


def place_rows(arrived, index):
    rows, width = arrived[0].shape
    slots = index.shape[0]
    count = min(slots, 512)
    return pl.pallas_call(
        place_kernel,
        grid_spec=pltpu.PrefetchScalarGridSpec(
            num_scalar_prefetch=1,
            grid=(slots // count,),
            in_specs=[pl.BlockSpec((rows, width), lambda t, i: (0, 0))] * len(arrived),
            out_specs=pl.BlockSpec((count, width), lambda t, i: (t, 0)),
            scratch_shapes=[pltpu.VMEM((rows * len(arrived), width), jnp.float32)],
        ),
        out_shape=jax.ShapeDtypeStruct((slots, width), jnp.float32),
        compiler_params=pltpu.CompilerParams(vmem_limit_bytes=VMEM_LIMIT),
        name="place_rows",
    )(index, *arrived)


def swap_columns(value, mask):
    columns = lax.axis_size("col")
    return lax.ppermute(value, "col", [(i, i ^ mask) for i in range(columns)])


def gram_terms(picked):
    half = picked.shape[0] // 2
    side = lax.axis_index("col") // 2

    def dot(a, b):
        return lax.dot_general(
            a, b, (((0,), (0,)), ((), ())), precision=lax.Precision.HIGH,
            preferred_element_type=jnp.float32,
        )

    mine = lax.dynamic_slice_in_dim(picked, side * half, half)
    theirs = lax.dynamic_slice_in_dim(picked, (1 - side) * half, half)
    across = swap_columns(theirs, 2)
    beside = swap_columns(picked, 1)
    diagonal = swap_columns(across, 1)
    beside_half = lax.dynamic_slice_in_dim(beside, side * half, half)
    near = dot(picked, jnp.concatenate([picked, beside], axis=1))
    far = dot(mine, jnp.concatenate([across, diagonal], axis=1))
    for_other = dot(across, jnp.concatenate([mine, beside_half], axis=1))
    return near, far, for_other


def gram_from(terms, sample_total, after):
    near, far, for_other = terms
    columns = lax.axis_size("col")
    c = lax.axis_index("col")
    width = near.shape[0]
    far = far + swap_columns(for_other, 2)
    blocks = jnp.concatenate([near, far], axis=1).reshape(width, columns, width)
    blocks = blocks.transpose(1, 0, 2)
    ordered = [lax.dynamic_index_in_dim(blocks, c ^ j, 0, keepdims=False) for j in range(columns)]
    partial = jnp.concatenate(ordered, axis=1)
    devices = lax.axis_size("row")
    if after is None or devices & (devices - 1) or width % (8 * devices):
        return sum_over_rows(partial) / sample_total
    return reduce_rows(partial, after, 1.0 / sample_total)


def reduce_kernel(scale, x_ref, *refs):
    out_ref, came, total, gathered, send_in, recv_in, send_out, recv_out = refs[-8:]
    devices = x_ref.shape[0]
    me = lax.axis_index("row")
    mesh_id = pl.DeviceIdType.MESH
    barrier = pltpu.get_barrier_semaphore()
    for m in range(1, devices):
        pl.semaphore_signal(barrier, inc=1, device_id={"row": me ^ m}, device_id_type=mesh_id)
    pl.semaphore_wait(barrier, devices - 1)
    copies = []
    for m in range(1, devices):
        copy = pltpu.make_async_remote_copy(
            src_ref=x_ref.at[me ^ m], dst_ref=came.at[m], send_sem=send_in.at[m],
            recv_sem=recv_in.at[m], device_id={"row": me ^ m}, device_id_type=mesh_id,
        )
        copy.start()
        copies.append(copy)
    value = x_ref[me]
    for m in range(1, devices):
        copies[m - 1].wait_recv()
        value = value + came[m]
    value = value * scale
    total[...] = value
    copies_out = []
    for m in range(1, devices):
        copy = pltpu.make_async_remote_copy(
            src_ref=total, dst_ref=gathered.at[m], send_sem=send_out.at[m],
            recv_sem=recv_out.at[m], device_id={"row": me ^ m}, device_id_type=mesh_id,
        )
        copy.start()
        copies_out.append(copy)
    out_ref[me] = value
    for m in range(1, devices):
        copies_out[m - 1].wait_recv()
        out_ref[me ^ m] = gathered[m]
    for copy in copies + copies_out:
        copy.wait_send()


def reduce_rows(partial, after, scale):
    devices = lax.axis_size("row")
    rows, columns = partial.shape
    part = (devices, rows // devices, columns)
    out = pl.pallas_call(
        functools.partial(reduce_kernel, scale),
        in_specs=[pl.BlockSpec(memory_space=pltpu.VMEM)]
        + [pl.BlockSpec(memory_space=pl.ANY)] * len(after),
        out_specs=pl.BlockSpec(memory_space=pltpu.VMEM),
        out_shape=jax.ShapeDtypeStruct(part, jnp.float32),
        scratch_shapes=[
            pltpu.VMEM(part, jnp.float32),
            pltpu.VMEM(part[1:], jnp.float32),
            pltpu.VMEM(part, jnp.float32),
        ]
        + [pltpu.SemaphoreType.DMA((devices,))] * 4,
        compiler_params=pltpu.CompilerParams(
            collective_id=0, has_side_effects=True, vmem_limit_bytes=VMEM_LIMIT
        ),
        name="reduce_rows",
    )(partial.reshape(part), *after)
    return out.reshape(rows, columns)


def sum_over_rows(value):
    devices = lax.axis_size("row")
    me = lax.axis_index("row")
    if devices & (devices - 1) or value.shape[0] % devices:
        return lax.psum(value, "row")

    def swap(part, mask):
        return lax.ppermute(part, "row", [(i, i ^ mask) for i in range(devices)])

    masks = [1 << k for k in range(devices.bit_length() - 1)]
    for mask in masks:
        half = value.shape[0] // 2
        upper = (me & mask) != 0
        low, high = value[:half], value[half:]
        value = jnp.where(upper, high, low) + swap(jnp.where(upper, low, high), mask)
    for mask in reversed(masks):
        upper = (me & mask) != 0
        other = swap(value, mask)
        low, high = jnp.where(upper, other, value), jnp.where(upper, value, other)
        value = jnp.concatenate([low, high], axis=0)
    return value


def shards(panel, signs, samples):
    row_count, width = panel.shape
    devices = lax.axis_size("row")
    members = devices // 2
    me = lax.axis_index("row")
    half, member = me // members, me % members
    outer = row_count // INNER
    block_len = row_count // devices
    sample_total = samples.shape[0]
    slots = sample_total // devices
    scale = 1.0 / math.sqrt(float(row_count * devices))
    groups = [list(range(members)), list(range(members, devices))]

    local_rows = local_transform(panel, signs, devices, 2, scale)
    pieces = [chunk.reshape(members, block_len, width) for chunk in local_rows]

    table = samples.reshape(devices, slots)
    local = table % row_count
    owners = (local // INNER) % devices
    in_block = (local // (INNER * devices)) * INNER + local % INNER
    flat = (table // row_count) * block_len + in_block
    ids = jnp.arange(devices, dtype=jnp.int32)
    onehot = owners[:, None, :] == ids[None, :, None]
    most = jnp.max(jnp.sum(onehot.astype(jnp.int32), axis=2))
    my_owners = lax.dynamic_index_in_dim(owners, me, 0, keepdims=False)
    my_onehot = my_owners[None, :] == ids[:, None]
    my_ranks = jnp.cumsum(my_onehot.astype(jnp.int32), axis=1) - 1
    position = jnp.sum(jnp.where(my_onehot, my_ranks, 0), axis=0)

    mean = slots / devices
    capacity = min(slots, -(-int(mean + 4.2 * math.sqrt(mean)) // 16) * 16)

    def pick_index(owner, room):
        mine = owners == owner
        rank = jnp.where(mine, jnp.cumsum(mine.astype(jnp.int32), axis=1) - 1, -1)
        wanted = jnp.arange(room, dtype=jnp.int32)[None, :, None]
        return jnp.sum(jnp.where(rank[:, None, :] == wanted, flat[:, None, :] + 8, 0), axis=2)

    def within(value):
        return lax.all_to_all(
            value, "row", split_axis=0, concat_axis=0, tiled=True, axis_index_groups=groups
        )

    def exchange_blocks(blocks):
        came = []
        for m in range(members):
            block = lax.dynamic_index_in_dim(blocks, member ^ m, 0, keepdims=False)
            if m:
                block = lax.ppermute(block, "row", [(i, i ^ m) for i in range(devices)])
            came.append(block)
        return came

    indices = [pick_index(k * members + member, capacity) for k in range(len(pieces))]
    first, *indices = lax.optimization_barrier((within(pieces[0]), *indices))

    def fast(*pieces):
        sign = 1 - 2 * half
        arrived, terms = [], None
        for k, piece in enumerate(pieces):
            received = within(piece) if k else first
            index = indices[k]
            picked = combine_and_pick(received, index, sign, capacity)
            kept = lax.dynamic_slice_in_dim(picked, half * members, members)
            sent = lax.dynamic_slice_in_dim(picked, (1 - half) * members, members)
            partner = [(i, (i + members) % devices) for i in range(devices)]
            came = lax.ppermute(sent, "row", partner)
            whole = add_blocks(kept, came, [*arrived, *terms]) if k else kept + came
            new = gram_terms(whole.reshape(members * capacity, width))
            terms = new if terms is None else [a + b for a, b in zip(terms, new)]
            arrived += exchange_blocks(whole)
        source = (my_owners // members) * members + ((my_owners % members) ^ member)
        sketch = place_rows(arrived, source * capacity + position)
        return sketch, gram_from(terms, sample_total, arrived)

    def general(*pieces):
        received = lax.all_to_all(
            jnp.concatenate(pieces), "row", split_axis=0, concat_axis=0, tiled=True
        )
        combined = jnp.stack(butterfly([received[d] for d in range(devices)]))
        combined = combined.reshape(devices * block_len, width)
        index = pick_index(me, slots).reshape(-1)
        picked = jnp.take(combined, jnp.maximum(index - 8, 0), axis=0)
        picked = jnp.where((index >= 8)[:, None], picked, 0.0)
        arrived = lax.all_to_all(
            picked.reshape(devices, slots, width), "row", split_axis=0, concat_axis=0, tiled=True
        )
        places = my_owners * slots + position
        sketch = jnp.take(arrived.reshape(devices * slots, width), places, axis=0)
        return sketch, gram_from(gram_terms(sketch), sample_total, None)

    return lax.cond(most <= capacity, fast, general, *pieces)


def solution(mesh):
    return jax.shard_map(
        shards,
        mesh=mesh,
        in_specs=(P("row", "col"), P("row"), P()),
        out_specs=(P("row", "col"), P("col", None)),
        check_vma=False,
    )
```
